256 devices in a mesh: dp: 8 (over y, core), code: 32 (over x, z).
Axes of the slice: x: 4, y: 4, z: 8, core: 2. Of those that a mesh axis runs over, the one named last changes fastest.
Arguments:
- cached_keys: bfloat16 [1048576, 128], P(('dp', 'code')), may hold values from -128 to 128
- codebook: float32 [65536, 128], P('code'), may hold values from -4 to 4
- block_lists: int32 [2048, 6], P(('dp', 'code')), may hold values from 0 to 255, as said below
- counts: int32 [2048], P(('dp', 'code')), may hold values from 2 to 6, as said below
Outputs:
- codebook_out: float32 [65536, 128], P('code')
- logsum: float32 [1048576], P(('dp', 'code'))
The draws below stay inside these ranges and needn't reach their ends.
Inputs may be any that keep to these rules, and one draw needn't show every extreme that they name: `block_lists`: within a row the first counts entries are distinct; entries past the count repeat the first. Owner o holds blocks o * (256 / the size of code) onward, consecutively; the key blocks of one device (aligned runs of 8 rows) name at most 1 distinct blocks of one owner, and in every draw one owner has exactly 1 named by every device. `counts`: some key block of every device lists 6 blocks.
All inputs are finite; a program needn't handle non-finite values.
Results may differ from the reference program's by a relative error of at most 0.0007.
Values sent between devices are 32-bit elements; how exact they have to be, the bound alone decides.
No kernel may reach another device: no remote copies, remote signals or barrier semaphores. Data moves between devices by JAX's collectives and lax.ppermute only.
A program may use at most 64 MiB of HBM per device.

```python
import jax
import jax.numpy as jnp
from jax import lax

H = 128
CODES = 65536
CBLK = 256
BLOCK = 512
LIST_MAX = 6
CAP = 1
ITERS = 2
KB_DEV = 8
KBLOCKS = 2048
KEYS = 1048576
CBLOCKS = 256
N_CODE = 32


def shared_codebook(key):
    base = jax.random.fold_in(key, 11)
    return jnp.clip(jax.random.normal(base, (CODES, H), jnp.float32), -4.0, 4.0)


def shared_lists(key):
    base = jax.random.fold_in(key, 23)
    device_count = KBLOCKS // KB_DEV
    own_blocks = CODES // CBLK // N_CODE
    width_slots = N_CODE * CAP
    first = jax.random.randint(jax.random.fold_in(base, 1), (device_count, N_CODE), 0, own_blocks)
    stride = jax.random.randint(jax.random.fold_in(base, 2), (device_count, N_CODE), 1, max(own_blocks // CAP, 2))
    local = (first[:, :, None] + jnp.arange(CAP, dtype=jnp.int32)[None, None, :] * stride[:, :, None]) % own_blocks
    owner_ids = jnp.arange(N_CODE, dtype=jnp.int32)[None, :, None]
    block_ids = (owner_ids * own_blocks + local).reshape(device_count, width_slots)
    hot_owner = jax.random.randint(jax.random.fold_in(base, 3), (), 0, N_CODE)
    coin = jax.random.randint(jax.random.fold_in(base, 4), (device_count, N_CODE, CAP), 0, 2)
    slot_pos = jnp.arange(CAP, dtype=jnp.int32)[None, None, :]
    is_hot = owner_ids == hot_owner
    usable = jnp.where((slot_pos == 0) | is_hot, 1, coin).reshape(device_count, width_slots)
    slot_index = jnp.arange(width_slots, dtype=jnp.int32)
    noise = jax.random.randint(jax.random.fold_in(base, 5), (device_count, KB_DEV, width_slots), 0, 1 << 20)
    ranking = noise * width_slots + slot_index[None, None, :]
    ranking = jnp.where(usable[:, None, :] == 1, ranking, -1 - slot_index[None, None, :])
    hot_flat = jnp.broadcast_to(is_hot, (1, N_CODE, CAP)).reshape(1, width_slots)
    first_row = (jnp.arange(KB_DEV, dtype=jnp.int32) == 0)[None, :, None]
    ranking = ranking + jnp.where(first_row & hot_flat[:, None, :], 1 << 28, 0)
    top_slots = lax.top_k(ranking, LIST_MAX)[1]
    picked = jnp.take_along_axis(jnp.broadcast_to(block_ids[:, None, :], (device_count, KB_DEV, width_slots)), top_slots, axis=2)
    counts = jax.random.randint(jax.random.fold_in(base, 6), (device_count, KB_DEV), 2, LIST_MAX + 1)
    counts = jnp.where(jnp.arange(KB_DEV, dtype=jnp.int32)[None, :] == 1, LIST_MAX, counts)
    within = jnp.arange(LIST_MAX, dtype=jnp.int32)[None, None, :] < counts[:, :, None]
    picked = jnp.where(within, picked, picked[:, :, 0:1])
    return (picked.reshape(KBLOCKS, LIST_MAX).astype(jnp.int32), counts.reshape(KBLOCKS).astype(jnp.int32))


def draw_codebook(key, part):
    return shared_codebook(key)


def draw_block_lists(key, part):
    return shared_lists(key)[0]


def draw_counts(key, part):
    return shared_lists(key)[1]


def draw_cached_keys(key, part):
    noise = jnp.clip(jax.random.normal(jax.random.fold_in(key, 13), (KEYS, H), jnp.float32), -4.0, 4.0)
    return noise.astype(jnp.bfloat16)


def setup_inputs(seed: int = 0) -> dict:
    splits = jax.random.split(jax.random.key(seed), 5)
    return {
        "cached_keys": draw_cached_keys(jax.random.fold_in(splits[4], 71), 0),
        "codebook": draw_codebook(jax.random.fold_in(splits[4], 71), 0),
        "block_lists": draw_block_lists(jax.random.fold_in(splits[4], 71), 0),
        "counts": draw_counts(jax.random.fold_in(splits[4], 71), 0),
    }


def reference(cached_keys, codebook, block_lists, counts):
    masked_score = -1e+30
    key_tiles = cached_keys.reshape(-1, BLOCK, H)
    listed_ok = jnp.arange(LIST_MAX)[None, :] < counts[:, None]
    current = codebook
    logsum = None
    for sweep in range(ITERS):
        code_full = current.reshape(CBLOCKS, CBLK, H)
        code_norm = lax.optimization_barrier(jnp.sum(current * current, axis=1)).reshape(CBLOCKS, CBLK)

        def one_block(running, block_item):
            total_sums, total_mass = running
            tile_keys, picked, listed = block_item
            word_rows = code_full[picked].reshape(-1, H)
            word_norms = code_norm[picked].reshape(-1)
            inner = lax.dot_general(tile_keys.astype(jnp.float32), word_rows, (((1,), (1,)), ((), ())), precision=lax.Precision.HIGHEST, preferred_element_type=jnp.float32)
            scores = (inner - 0.5 * word_norms[None, :]) / jnp.sqrt(jnp.float32(H))
            column_live = jnp.repeat(listed, CBLK)
            scores = jnp.where(column_live[None, :], scores, masked_score)
            row_top = lax.optimization_barrier(jnp.max(scores, axis=1, keepdims=True))
            unnorm = jnp.exp(scores - row_top)
            row_total = lax.optimization_barrier(jnp.sum(unnorm, axis=1, keepdims=True))
            row_logsum = row_top[:, 0] + jnp.log(row_total[:, 0])
            posterior = (unnorm / row_total).astype(jnp.bfloat16)
            weighted = lax.dot_general(posterior, tile_keys, (((0,), (0,)), ((), ())), preferred_element_type=jnp.float32)
            weight = lax.optimization_barrier(jnp.sum(posterior.astype(jnp.float32), axis=0))
            total_sums = total_sums.at[picked].add(weighted.reshape(LIST_MAX, CBLK, H))
            total_mass = total_mass.at[picked].add(weight.reshape(LIST_MAX, CBLK))
            return ((total_sums, total_mass), row_logsum)
        start_state = (jnp.zeros((CBLOCKS, CBLK, H), jnp.float32), jnp.zeros((CBLOCKS, CBLK), jnp.float32))
        (total_sums, total_mass), logsum = lax.scan(one_block, start_state, (key_tiles, block_lists, listed_ok))
        current = (total_sums.reshape(CODES, H) + current) / (total_mass.reshape(CODES)[:, None] + 1.0)
    return (current, logsum.reshape(-1))
```

```python
import functools
import math

import jax
import jax.numpy as jnp
from jax import lax
from jax.experimental import pallas as pl
from jax.experimental.pallas import tpu as pltpu
from jax.sharding import PartitionSpec as P

CBLK = 256
HALF = CBLK // 2
LIST_MAX = 6
ITERS = 2
BLOCK = 512
H = 128
NX, NZ, NY = 4, 8, 4
NDP = 8
NCODE = NX * NZ
KB_DEV = 8
KB_ALL = NDP * KB_DEV
ENTRIES = KB_ALL * LIST_MAX
ROWS = HALF + 8
SCALE = math.log2(math.e) / math.sqrt(H)
LN2 = math.log(2.0)
LOW = -1e30


def x_step(v, k):
    pairs = [(x * NZ + z, (x + k) % NX * NZ + z) for x in range(NX) for z in range(NZ)]
    return lax.ppermute(v, "code", pairs)


def z_step(v, k):
    pairs = [(x * NZ + z, x * NZ + (z + k) % NZ) for x in range(NX) for z in range(NZ)]
    return lax.ppermute(v, "code", pairs)


def ring_gather(v, n, step):
    h = v.shape[0] // 2
    far = n // 2
    parts = [None] * n
    parts[0] = v
    up, down = v, v
    for s in range(1, far):
        up, down = step(up, 1), step(down, -1)
        parts[n - s], parts[s] = up, down
    a, b = step(up[:h], 1), step(down[h:], -1)
    parts[far] = jnp.concatenate([a, b], 0)
    return parts


def ring_reduce(terms, n, step):
    far = n // 2
    h = terms[0].shape[0] // 2
    a, b = step(terms[far][:h], 1), step(terms[far][h:], -1)
    up = jnp.concatenate([terms[far - 1][:h] + a, terms[far - 1][h:]], 0)
    down = jnp.concatenate([terms[n - far + 1][:h], terms[n - far + 1][h:] + b], 0)
    for s in range(far - 1, 0, -1):
        a, b = step(up, 1), step(down, -1)
        if s > 1:
            up, down = terms[s - 1] + a, terms[n - s + 1] + b
    return terms[0] + a + b


def gather_words(block):
    top, low = block[:HALF], block[HALF:]
    with jax.named_scope("gather_top"):
        mine = jnp.concatenate([top, x_step(top, -1), x_step(top, 2), x_step(top, 1)], 0)
        tops = jnp.concatenate(ring_gather(mine, NZ, z_step), 0)
    with jax.named_scope("gather_low"):
        mine = jnp.concatenate(ring_gather(low, NZ, z_step), 0)
        lows = jnp.concatenate(ring_gather(mine, NX, x_step), 0)
    return tops.reshape(NCODE, HALF, H), lows.reshape(NCODE, HALF, H)


def reduce_sums(tops, lows):
    with jax.named_scope("reduce_top"):
        r = ring_reduce([tops[j].reshape(NX * ROWS, H) for j in range(NZ)], NZ, z_step)
        r = r.reshape(NX, ROWS, H)
        top = r[0] + x_step(r[1], 1) + x_step(r[2], 2) + x_step(r[3], -1)
    with jax.named_scope("reduce_low"):
        r = ring_reduce([lows[i].reshape(NZ * ROWS, H) for i in range(NX)], NX, x_step)
        r = r.reshape(NZ, ROWS, H)
        low = ring_reduce([r[j] for j in range(NZ)], NZ, z_step)
    return top, low


def dp_swap(v):
    return lax.all_to_all(v, "dp", split_axis=0, concat_axis=0, tiled=True)


def pair_of(word):
    kb = word // NCODE
    slot = word % NCODE
    return kb, slot, slot % NX * NZ + slot // NX


def copies(pairs, keys_hbm, tops_hbm, lows_hbm, kbuf, cbuf, sem, p):
    kb, top, low = pair_of(pairs[p])
    at = p % 2
    return (
        pltpu.make_async_copy(keys_hbm.at[kb], kbuf.at[at], sem.at[0, at]),
        pltpu.make_async_copy(tops_hbm.at[top], cbuf.at[at, pl.ds(0, HALF)], sem.at[1, at]),
        pltpu.make_async_copy(lows_hbm.at[low], cbuf.at[at, pl.ds(HALF, HALF)], sem.at[2, at]),
    )


def over_pairs(pairs, count, hbm, bufs, sem, work):
    n = count[0]

    @pl.when(n > 0)
    def _():
        for c in copies(pairs, *hbm, *bufs, sem, 0):
            c.start()

    @pl.loop(0, n)
    def _(p):
        @pl.when(p + 1 < n)
        def _():
            for c in copies(pairs, *hbm, *bufs, sem, p + 1):
                c.start()

        for c in copies(pairs, *hbm, *bufs, sem, p):
            c.wait()
        work(p)


def split_words(c):
    norm = jnp.sum(c * c, axis=1, keepdims=True) * (0.5 * SCALE)
    s = c * SCALE
    hi = s.astype(jnp.bfloat16)
    rest = s - hi.astype(jnp.float32)
    mid = rest.astype(jnp.bfloat16)
    low = (rest - mid.astype(jnp.float32)).astype(jnp.bfloat16)
    return jnp.concatenate([hi, mid], 1), low, norm


def scores_of(words, k):
    two, low, norm = words
    nt = (((1,), (1,)), ((), ()))
    s = lax.dot_general(two, jnp.concatenate([k, k], 1), nt, preferred_element_type=jnp.float32)
    s += lax.dot_general(low, k, nt, preferred_element_type=jnp.float32)
    return s - norm


def logsum_kernel(pairs, count, keys_hbm, tops_hbm, lows_hbm, out, kbuf, cbuf, top_ref, sum_ref, sem):
    top_ref[...] = jnp.full_like(top_ref, LOW)
    sum_ref[...] = jnp.zeros_like(sum_ref)

    def work(p):
        kb = pairs[p] // NCODE
        at = p % 2
        words = split_words(cbuf[at])
        for part in range(2):
            cols = pl.ds(part * 256, 256)
            s = scores_of(words, kbuf[at, cols, :].astype(jnp.bfloat16))
            old = top_ref[pl.ds(kb, 1), cols]
            top = jnp.maximum(old, jnp.max(s, axis=0, keepdims=True))
            total = jnp.sum(jnp.exp2(s - top), axis=0, keepdims=True)
            sum_ref[pl.ds(kb, 1), cols] = sum_ref[pl.ds(kb, 1), cols] * jnp.exp2(old - top) + total
            top_ref[pl.ds(kb, 1), cols] = top

    over_pairs(pairs, count, (keys_hbm, tops_hbm, lows_hbm), (kbuf, cbuf), sem, work)
    total = sum_ref[...]
    out[...] = jnp.where(total > 0.0, top_ref[...] + jnp.log2(total), LOW)


def sums_kernel(pairs, count, keys_hbm, tops_hbm, lows_hbm, lse, tops_out, lows_out, kbuf, cbuf, acc, sem):
    tops_out[...] = jnp.zeros_like(tops_out)
    lows_out[...] = jnp.zeros_like(lows_out)
    acc[...] = jnp.zeros_like(acc)

    def work(p):
        kb, top, low = pair_of(pairs[p])
        at = p % 2
        words = split_words(cbuf[at])
        both = None
        for part in range(2):
            cols = pl.ds(part * 256, 256)
            k = kbuf[at, cols, :].astype(jnp.bfloat16)
            s = scores_of(words, k)
            post = jnp.exp2(s - lse[pl.ds(kb, 1), cols]).astype(jnp.bfloat16)
            wide = jnp.concatenate([k, jnp.ones_like(k)], 1)
            d = jnp.dot(post, wide, preferred_element_type=jnp.float32)
            both = d if both is None else both + d
        tops_out[top, pl.ds(0, HALF), :] += both[:HALF, :H]
        lows_out[low, pl.ds(0, HALF), :] += both[HALF:, :H]
        acc[top] += both[:, H:]

    over_pairs(pairs, count, (keys_hbm, tops_hbm, lows_hbm), (kbuf, cbuf), sem, work)
    rows = lax.broadcasted_iota(jnp.int32, (HALF, H), 0)
    lanes = lax.broadcasted_iota(jnp.int32, (HALF, H), 1)
    diag = rows == lanes
    for slot in range(NCODE):
        m = acc[slot]
        other = slot % NX * NZ + slot // NX
        a = jnp.sum(jnp.where(diag, m[:HALF], 0.0), axis=0, keepdims=True)
        b = jnp.sum(jnp.where(diag, m[HALF:], 0.0), axis=0, keepdims=True)
        tops_out[slot, pl.ds(HALF, 8), :] = jnp.broadcast_to(a, (8, H))
        lows_out[other, pl.ds(HALF, 8), :] = jnp.broadcast_to(b, (8, H))


PARAMS = pltpu.CompilerParams(vmem_limit_bytes=48 * 2**20)
SMEM = pl.BlockSpec(memory_space=pltpu.SMEM)
VMEM = pl.BlockSpec(memory_space=pltpu.VMEM)
ANY = pl.BlockSpec(memory_space=pl.ANY)
BUFS = [pltpu.VMEM((2, BLOCK, H), jnp.float32), pltpu.VMEM((2, CBLK, H), jnp.float32)]


def local_logsum(pairs, count, keys, tops, lows):
    return pl.pallas_call(
        logsum_kernel,
        out_shape=jax.ShapeDtypeStruct((KB_ALL, BLOCK), jnp.float32),
        in_specs=[SMEM, SMEM, ANY, ANY, ANY],
        out_specs=VMEM,
        scratch_shapes=BUFS
        + [
            pltpu.VMEM((KB_ALL, BLOCK), jnp.float32),
            pltpu.VMEM((KB_ALL, BLOCK), jnp.float32),
            pltpu.SemaphoreType.DMA((3, 2)),
        ],
        compiler_params=PARAMS,
        name="local_logsum",
    )(pairs, count, keys, tops, lows)


def local_sums(pairs, count, keys, tops, lows, lse):
    shape = jax.ShapeDtypeStruct((NCODE, ROWS, H), jnp.float32)
    return pl.pallas_call(
        sums_kernel,
        out_shape=(shape, shape),
        in_specs=[SMEM, SMEM, ANY, ANY, ANY, VMEM],
        out_specs=(VMEM, VMEM),
        scratch_shapes=BUFS
        + [pltpu.VMEM((NCODE, CBLK, H), jnp.float32), pltpu.SemaphoreType.DMA((3, 2))],
        compiler_params=PARAMS,
        name="local_sums",
    )(pairs, count, keys, tops, lows, lse)


def list_pairs(ids, counts, d, x, z):
    kb = lax.broadcasted_iota(jnp.int32, (KB_ALL, LIST_MAX), 0)
    place = lax.broadcasted_iota(jnp.int32, (KB_ALL, LIST_MAX), 1)
    owner = ids // NDP
    take = ((place < counts[:, None]) & (ids % NDP == d)).reshape(-1)
    slot = (owner % NZ - z) % NZ * NX + (owner // NZ - x) % NX
    word = (kb * NCODE + slot).reshape(-1)
    index = jnp.arange(ENTRIES, dtype=jnp.int32)
    ahead = jnp.sum((take[:, None] & (index[:, None] < index[None, :])).astype(jnp.int32), axis=0)
    here = take[:, None] & (ahead[:, None] == index[None, :])
    pairs = jnp.sum(jnp.where(here, word[:, None], 0), axis=0)
    return pairs, jnp.sum(take.astype(jnp.int32)).reshape(1)


def on_device(cached_keys, codebook, block_lists, counts):
    d = lax.axis_index("dp")
    code = lax.axis_index("code")
    x, z = code // NZ, code % NZ
    keys = lax.all_gather(cached_keys.astype(jnp.float32), "dp", axis=0, tiled=True)
    keys = keys.reshape(KB_ALL, BLOCK, H)
    entry = jnp.concatenate([block_lists, counts[:, None], counts[:, None]], 1)
    entries = dp_swap(jnp.broadcast_to(entry[None], (NDP, KB_DEV, 8))).reshape(KB_ALL, 8)
    pairs, count = list_pairs(entries[:, :LIST_MAX], entries[:, LIST_MAX], d, x, z)
    current = lax.dynamic_slice_in_dim(codebook, d * CBLK, CBLK, 0)
    for sweep in range(ITERS):
        tops, lows = gather_words(current)
        part = local_logsum(pairs, count, keys, tops, lows)
        part = dp_swap(part.reshape(NDP, KB_DEV, BLOCK))
        peak = jnp.max(part, axis=0)
        own = peak + jnp.log2(jnp.sum(jnp.exp2(part - peak[None]), axis=0))
        lse = dp_swap(jnp.broadcast_to(own[None], (NDP, KB_DEV, BLOCK))).reshape(KB_ALL, BLOCK)
        tops, lows = local_sums(pairs, count, keys, tops, lows, lse)
        top, low = reduce_sums(
            tops.reshape(NZ, NX, ROWS, H), lows.reshape(NX, NZ, ROWS, H)
        )
        sums = jnp.concatenate([top[:HALF], low[:HALF]], 0)
        mass = jnp.concatenate([top[HALF], low[HALF]], 0)
        current = (sums + current) / (mass[:, None] + 1.0)
    book = dp_swap(jnp.broadcast_to(current[None], (NDP, CBLK, H))).reshape(NDP * CBLK, H)
    return book, (own * LN2).reshape(-1)


def solution(mesh):
    in_specs = (
        P(("dp", "code"), None),
        P("code", None),
        P(("dp", "code"), None),
        P(("dp", "code")),
    )
    out_specs = (P("code", None), P(("dp", "code")))
    return jax.shard_map(
        on_device, mesh=mesh, in_specs=in_specs, out_specs=out_specs, check_vma=False
    )
```

```python
import math

import jax
import jax.numpy as jnp
from jax import lax
from jax.experimental import pallas as pl
from jax.experimental.pallas import tpu as pltpu
from jax.sharding import PartitionSpec as P

CBLK = 256
HALF = CBLK // 2
LIST_MAX = 6
ITERS = 2
BLOCK = 512
H = 128
NX, NZ, NY = 4, 8, 4
NDP = 8
NCODE = NX * NZ
KB_DEV = 8
KB_ALL = NDP * KB_DEV
ENTRIES = KB_ALL * LIST_MAX
ROWS = HALF + 8
SCALE = math.log2(math.e) / math.sqrt(H)
LN2 = math.log(2.0)
LOW = -1e30


def x_step(v, k):
    pairs = [(x * NZ + z, (x + k) % NX * NZ + z) for x in range(NX) for z in range(NZ)]
    return lax.ppermute(v, "code", pairs)


def z_step(v, k):
    pairs = [(x * NZ + z, x * NZ + (z + k) % NZ) for x in range(NX) for z in range(NZ)]
    return lax.ppermute(v, "code", pairs)


def ring_gather(v, n, step):
    h = v.shape[0] // 2
    far = n // 2
    parts = [None] * n
    parts[0] = v
    up, down = v, v
    for s in range(1, far):
        up, down = step(up, 1), step(down, -1)
        parts[n - s], parts[s] = up, down
    a, b = step(up[:h], 1), step(down[h:], -1)
    parts[far] = jnp.concatenate([a, b], 0)
    return parts


def ring_reduce(terms, n, step):
    far = n // 2
    h = terms[0].shape[0] // 2
    a, b = step(terms[far][:h], 1), step(terms[far][h:], -1)
    up = jnp.concatenate([terms[far - 1][:h] + a, terms[far - 1][h:]], 0)
    down = jnp.concatenate([terms[n - far + 1][:h], terms[n - far + 1][h:] + b], 0)
    for s in range(far - 1, 0, -1):
        a, b = step(up, 1), step(down, -1)
        if s > 1:
            up, down = terms[s - 1] + a, terms[n - s + 1] + b
    return terms[0] + a + b


def gather_words(block):
    top, low = block[:HALF], block[HALF:]
    with jax.named_scope("gather_top"):
        mine = jnp.concatenate([top, x_step(top, -1), x_step(top, 2), x_step(top, 1)], 0)
        tops = jnp.concatenate(ring_gather(mine, NZ, z_step), 0)
    with jax.named_scope("gather_low"):
        mine = jnp.concatenate(ring_gather(low, NZ, z_step), 0)
        lows = jnp.concatenate(ring_gather(mine, NX, x_step), 0)
    return tops.reshape(NCODE, HALF, H), lows.reshape(NCODE, HALF, H)


def reduce_sums(tops, lows):
    with jax.named_scope("reduce_top"):
        r = ring_reduce([tops[j].reshape(NX * ROWS, H) for j in range(NZ)], NZ, z_step)
        r = r.reshape(NX, ROWS, H)
        top = r[0] + x_step(r[1], 1) + x_step(r[2], 2) + x_step(r[3], -1)
    with jax.named_scope("reduce_low"):
        r = ring_reduce([lows[i].reshape(NZ * ROWS, H) for i in range(NX)], NX, x_step)
        r = r.reshape(NZ, ROWS, H)
        low = ring_reduce([r[j] for j in range(NZ)], NZ, z_step)
    return top, low


def dp_swap(v):
    return lax.all_to_all(v, "dp", split_axis=0, concat_axis=0, tiled=True)


UNROLL = 4
PREP = 2


def low_slot(slot):
    return slot % NX * NZ + slot // NX


def three_terms(v):
    hi = v.astype(jnp.bfloat16)
    rest = v - hi.astype(jnp.float32)
    mid = rest.astype(jnp.bfloat16)
    return hi, mid, (rest - mid.astype(jnp.float32)).astype(jnp.bfloat16)


def fill_words(tops, lows, words):
    lane = lax.broadcasted_iota(jnp.int32, (HALF, H), 1)

    @pl.loop(0, NCODE // PREP)
    def _(step):
        for u in range(PREP):
            slot = step * PREP + u
            for half, c in enumerate((tops[slot], lows[low_slot(slot)])):
                rows = pl.ds(half * HALF, HALF)
                for i, t in enumerate(three_terms(c * SCALE)):
                    words[slot, rows, i * H : (i + 1) * H] = t
                norm = jnp.sum(c * c, axis=1, keepdims=True) * (-0.5 * SCALE)
                n0, n1, n2 = (t.astype(jnp.float32) for t in three_terms(norm))
                n = jnp.where(lane == 0, n0, jnp.where(lane == 1, n1, jnp.where(lane == 2, n2, 0.0)))
                words[slot, rows, 3 * H :] = n.astype(jnp.bfloat16)


def scores_of(words, k, ones):
    wide = jnp.concatenate([k, k, k, ones], 1)
    return lax.dot_general(words, wide, (((1,), (1,)), ((), ())), preferred_element_type=jnp.float32)


def pair_loop(pairs, count, keys_hbm, kbuf, sem, work):
    n = count[0]
    steps = (n + (UNROLL - 1)) // UNROLL

    def fetch(step, u):
        at = (step % 2) * UNROLL + u
        kb = pairs[step * UNROLL + u] // NCODE
        return pltpu.make_async_copy(keys_hbm.at[kb], kbuf.at[at], sem.at[at])

    def begin():
        @pl.when(n > 0)
        def _():
            for u in range(UNROLL):
                fetch(0, u).start()

    def run():
        @pl.loop(0, steps)
        def _(step):
            @pl.when(step + 1 < steps)
            def _():
                for u in range(UNROLL):
                    fetch(step + 1, u).start()

            for u in range(UNROLL):
                fetch(step, u).wait()
            work([(step * UNROLL + u, (step % 2) * UNROLL + u) for u in range(UNROLL)], n)

    return begin, run


def logsum_kernel(pairs, count, keys_hbm, tops, lows, out, words, kbuf, top_ref, sum_ref, sem):
    def work(items, n):
        found = []
        for p, at in items:
            k = kbuf[at].astype(jnp.bfloat16)
            s = scores_of(words[pairs[p] % NCODE], k, jnp.ones_like(k))
            peak = jnp.max(s, axis=0, keepdims=True)
            found.append((peak, jnp.sum(jnp.exp2(s - peak), axis=0, keepdims=True)))
        for (p, _), (peak, total) in zip(items, found):
            kb = pl.ds(jnp.where(p < n, pairs[p] // NCODE, KB_ALL), 1)
            old = top_ref[kb, :]
            top = jnp.maximum(old, peak)
            sum_ref[kb, :] = sum_ref[kb, :] * jnp.exp2(old - top) + total * jnp.exp2(peak - top)
            top_ref[kb, :] = top

    begin, run = pair_loop(pairs, count, keys_hbm, kbuf, sem, work)
    begin()
    top_ref[...] = jnp.full_like(top_ref, LOW)
    sum_ref[...] = jnp.zeros_like(sum_ref)
    fill_words(tops, lows, words)
    run()
    total = sum_ref[:KB_ALL, :]
    out[...] = jnp.where(total > 0.0, top_ref[:KB_ALL, :] + jnp.log2(total), LOW)


def sums_kernel(pairs, count, keys_hbm, words, lse, tops_out, lows_out, kbuf, acc, sem):
    def work(items, n):
        found = []
        for p, at in items:
            k = kbuf[at].astype(jnp.bfloat16)
            ones = jnp.ones_like(k)
            s = scores_of(words[pairs[p] % NCODE], k, ones)
            post = jnp.exp2(s - lse[pl.ds(pairs[p] // NCODE, 1), :]).astype(jnp.bfloat16)
            wide = jnp.concatenate([k, ones], 1)
            found.append(jnp.dot(post, wide, preferred_element_type=jnp.float32))
        for (p, _), both in zip(items, found):
            acc[jnp.where(p < n, pairs[p] % NCODE, NCODE)] += both

    begin, run = pair_loop(pairs, count, keys_hbm, kbuf, sem, work)
    begin()
    acc[...] = jnp.zeros_like(acc)
    run()
    rows = lax.broadcasted_iota(jnp.int32, (HALF, H), 0)
    lanes = lax.broadcasted_iota(jnp.int32, (HALF, H), 1)
    diag = rows == lanes
    for slot in range(NCODE):
        for half, (ref, to) in enumerate(((tops_out, slot), (lows_out, low_slot(slot)))):
            part = acc[slot, half * HALF : (half + 1) * HALF, :]
            ref[to, :HALF, :] = part[:, :H]
            mass = jnp.sum(jnp.where(diag, part[:, H:], 0.0), axis=0, keepdims=True)
            ref[to, HALF:, :] = jnp.broadcast_to(mass, (8, H))


SMEM = pl.BlockSpec(memory_space=pltpu.SMEM)
VMEM = pl.BlockSpec(memory_space=pltpu.VMEM)
ANY = pl.BlockSpec(memory_space=pl.ANY)
KBUF = pltpu.VMEM((2 * UNROLL, BLOCK, H), jnp.float32)
KSEM = pltpu.SemaphoreType.DMA((2 * UNROLL,))


def local_logsum(pairs, count, keys, tops, lows):
    return pl.pallas_call(
        logsum_kernel,
        out_shape=(
            jax.ShapeDtypeStruct((KB_ALL, BLOCK), jnp.float32),
            jax.ShapeDtypeStruct((NCODE, CBLK, 4 * H), jnp.bfloat16),
        ),
        in_specs=[SMEM, SMEM, ANY, VMEM, VMEM],
        out_specs=(VMEM, VMEM),
        scratch_shapes=[
            KBUF,
            pltpu.VMEM((KB_ALL + 8, BLOCK), jnp.float32),
            pltpu.VMEM((KB_ALL + 8, BLOCK), jnp.float32),
            KSEM,
        ],
        compiler_params=pltpu.CompilerParams(vmem_limit_bytes=32 * 2**20),
        name="local_logsum",
    )(pairs, count, keys, tops, lows)


def local_sums(pairs, count, keys, words, lse):
    shape = jax.ShapeDtypeStruct((NCODE, ROWS, H), jnp.float32)
    return pl.pallas_call(
        sums_kernel,
        out_shape=(shape, shape),
        in_specs=[SMEM, SMEM, ANY, VMEM, VMEM],
        out_specs=(VMEM, VMEM),
        scratch_shapes=[KBUF, pltpu.VMEM((NCODE + 1, CBLK, 2 * H), jnp.float32), KSEM],
        compiler_params=pltpu.CompilerParams(vmem_limit_bytes=40 * 2**20),
        name="local_sums",
    )(pairs, count, keys, words, lse)


def list_pairs(ids, counts, d, x, z):
    kb = lax.broadcasted_iota(jnp.int32, (KB_ALL, LIST_MAX), 0)
    place = lax.broadcasted_iota(jnp.int32, (KB_ALL, LIST_MAX), 1)
    owner = ids // NDP
    take = ((place < counts[:, None]) & (ids % NDP == d)).reshape(-1)
    slot = (owner % NZ - z) % NZ * NX + (owner // NZ - x) % NX
    word = (kb * NCODE + slot).reshape(-1)
    index = jnp.arange(ENTRIES, dtype=jnp.int32)
    ahead = jnp.sum((take[:, None] & (index[:, None] < index[None, :])).astype(jnp.int32), axis=0)
    here = take[:, None] & (ahead[:, None] == index[None, :])
    pairs = jnp.sum(jnp.where(here, word[:, None], 0), axis=0)
    return pairs, jnp.sum(take.astype(jnp.int32)).reshape(1)


def on_device(cached_keys, codebook, block_lists, counts):
    d = lax.axis_index("dp")
    code = lax.axis_index("code")
    x, z = code // NZ, code % NZ
    keys = lax.all_gather(cached_keys.astype(jnp.float32), "dp", axis=0, tiled=True)
    keys = keys.reshape(KB_ALL, BLOCK, H)
    entry = jnp.concatenate([block_lists, counts[:, None], counts[:, None]], 1)
    entries = dp_swap(jnp.broadcast_to(entry[None], (NDP, KB_DEV, 8))).reshape(KB_ALL, 8)
    pairs, count = list_pairs(entries[:, :LIST_MAX], entries[:, LIST_MAX], d, x, z)
    current = lax.dynamic_slice_in_dim(codebook, d * CBLK, CBLK, 0)
    for sweep in range(ITERS):
        tops, lows = gather_words(current)
        part, words = local_logsum(pairs, count, keys, tops, lows)
        part = dp_swap(part.reshape(NDP, KB_DEV, BLOCK))
        peak = jnp.max(part, axis=0)
        own = peak + jnp.log2(jnp.sum(jnp.exp2(part - peak[None]), axis=0))
        lse = dp_swap(jnp.broadcast_to(own[None], (NDP, KB_DEV, BLOCK))).reshape(KB_ALL, BLOCK)
        tops, lows = local_sums(pairs, count, keys, words, lse)
        top, low = reduce_sums(
            tops.reshape(NZ, NX, ROWS, H), lows.reshape(NX, NZ, ROWS, H)
        )
        sums = jnp.concatenate([top[:HALF], low[:HALF]], 0)
        mass = jnp.concatenate([top[HALF], low[HALF]], 0)
        current = (sums + current) / (mass[:, None] + 1.0)
    book = dp_swap(jnp.broadcast_to(current[None], (NDP, CBLK, H))).reshape(NDP * CBLK, H)
    return book, (own * LN2).reshape(-1)


def solution(mesh):
    in_specs = (
        P(("dp", "code"), None),
        P("code", None),
        P(("dp", "code"), None),
        P(("dp", "code")),
    )
    out_specs = (P("code", None), P(("dp", "code")))
    return jax.shard_map(
        on_device, mesh=mesh, in_specs=in_specs, out_specs=out_specs, check_vma=False
    )
```

```python
import math

import jax
import jax.numpy as jnp
from jax import lax
from jax.experimental import pallas as pl
from jax.experimental.pallas import tpu as pltpu
from jax.sharding import PartitionSpec as P

CBLK = 256
HALF = CBLK // 2
LIST_MAX = 6
ITERS = 2
BLOCK = 512
H = 128
NX, NZ, NY = 4, 8, 4
NDP = 8
NCODE = NX * NZ
KB_DEV = 8
KB_ALL = NDP * KB_DEV
ENTRIES = KB_ALL * LIST_MAX
ROWS = HALF + 8
SCALE = math.log2(math.e) / math.sqrt(H)
LN2 = math.log(2.0)
LOW = -1e30


def x_step(v, k):
    pairs = [(x * NZ + z, (x + k) % NX * NZ + z) for x in range(NX) for z in range(NZ)]
    return lax.ppermute(v, "code", pairs)


def z_step(v, k):
    pairs = [(x * NZ + z, x * NZ + (z + k) % NZ) for x in range(NX) for z in range(NZ)]
    return lax.ppermute(v, "code", pairs)


def ring_gather(v, n, step):
    h = v.shape[0] // 2
    far = n // 2
    parts = [None] * n
    parts[0] = v
    up, down = v, v
    for s in range(1, far):
        up, down = step(up, 1), step(down, -1)
        parts[n - s], parts[s] = up, down
    a, b = step(up[:h], 1), step(down[h:], -1)
    parts[far] = jnp.concatenate([a, b], 0)
    return parts


def ring_reduce(terms, n, step):
    far = n // 2
    h = terms[0].shape[0] // 2
    a, b = step(terms[far][:h], 1), step(terms[far][h:], -1)
    up = jnp.concatenate([terms[far - 1][:h] + a, terms[far - 1][h:]], 0)
    down = jnp.concatenate([terms[n - far + 1][:h], terms[n - far + 1][h:] + b], 0)
    for s in range(far - 1, 0, -1):
        a, b = step(up, 1), step(down, -1)
        if s > 1:
            up, down = terms[s - 1] + a, terms[n - s + 1] + b
    return terms[0] + a + b


def gather_words(block):
    top, low = block[:HALF], block[HALF:]
    with jax.named_scope("gather_top"):
        mine = jnp.concatenate([top, x_step(top, -1), x_step(top, 2), x_step(top, 1)], 0)
        tops = jnp.concatenate(ring_gather(mine, NZ, z_step), 0)
    with jax.named_scope("gather_low"):
        mine = jnp.concatenate(ring_gather(low, NZ, z_step), 0)
        lows = jnp.concatenate(ring_gather(mine, NX, x_step), 0)
    return tops.reshape(NCODE, HALF, H), lows.reshape(NCODE, HALF, H)


def reduce_sums(tops, lows):
    with jax.named_scope("reduce_top"):
        r = ring_reduce([tops[j].reshape(NX * ROWS, H) for j in range(NZ)], NZ, z_step)
        r = r.reshape(NX, ROWS, H)
        top = r[0] + x_step(r[1], 1) + x_step(r[2], 2) + x_step(r[3], -1)
    with jax.named_scope("reduce_low"):
        r = ring_reduce([lows[i].reshape(NZ * HALF, H) for i in range(NX)], NX, x_step)
        r = r.reshape(NZ, HALF, H)
        low = ring_reduce([r[j] for j in range(NZ)], NZ, z_step)
    return top, low


def dp_swap(v):
    return lax.all_to_all(v, "dp", split_axis=0, concat_axis=0, tiled=True)


UNROLL = 4
PREP = 2


def low_slot(slot):
    return slot % NX * NZ + slot // NX


def three_terms(v):
    hi = v.astype(jnp.bfloat16)
    rest = v - hi.astype(jnp.float32)
    mid = rest.astype(jnp.bfloat16)
    return hi, mid, (rest - mid.astype(jnp.float32)).astype(jnp.bfloat16)


def fill_words(tops, lows, words):
    lane = lax.broadcasted_iota(jnp.int32, (HALF, H), 1)

    @pl.loop(0, NCODE // PREP)
    def _(step):
        for u in range(PREP):
            slot = step * PREP + u
            for half, c in enumerate((tops[slot], lows[low_slot(slot)])):
                rows = pl.ds(half * HALF, HALF)
                for i, t in enumerate(three_terms(c * SCALE)):
                    words[slot, rows, i * H : (i + 1) * H] = t
                norm = jnp.sum(c * c, axis=1, keepdims=True) * (-0.5 * SCALE)
                n0, n1, n2 = (t.astype(jnp.float32) for t in three_terms(norm))
                n = jnp.where(lane == 0, n0, jnp.where(lane == 1, n1, jnp.where(lane == 2, n2, 0.0)))
                words[slot, rows, 3 * H :] = n.astype(jnp.bfloat16)


def scores_of(words, k, ones):
    wide = jnp.concatenate([k, k, k, ones], 1)
    return lax.dot_general(words, wide, (((1,), (1,)), ((), ())), preferred_element_type=jnp.float32)


def pair_loop(pairs, count, keys_hbm, kbuf, sem, work):
    n = count[0]
    steps = (n + (UNROLL - 1)) // UNROLL

    def fetch(step, u):
        at = (step % 2) * UNROLL + u
        kb = pairs[step * UNROLL + u] // NCODE
        return pltpu.make_async_copy(keys_hbm.at[kb], kbuf.at[at], sem.at[at])

    def begin():
        @pl.when(n > 0)
        def _():
            for u in range(UNROLL):
                fetch(0, u).start()

    def run():
        @pl.loop(0, steps)
        def _(step):
            @pl.when(step + 1 < steps)
            def _():
                for u in range(UNROLL):
                    fetch(step + 1, u).start()

            for u in range(UNROLL):
                fetch(step, u).wait()
            work([(step * UNROLL + u, (step % 2) * UNROLL + u) for u in range(UNROLL)], n)

    return begin, run


def logsum_kernel(pairs, count, keys_hbm, tops, lows, out, words, kbuf, top_ref, sum_ref, sem):
    def work(items, n):
        found = []
        for p, at in items:
            k = kbuf[at].astype(jnp.bfloat16)
            s = scores_of(words[pairs[p] % NCODE], k, jnp.ones_like(k))
            peak = jnp.max(s, axis=0, keepdims=True)
            found.append((peak, jnp.sum(jnp.exp2(s - peak), axis=0, keepdims=True)))
        for (p, _), (peak, total) in zip(items, found):
            kb = pl.ds(jnp.where(p < n, pairs[p] // NCODE, KB_ALL), 1)
            old = top_ref[kb, :]
            top = jnp.maximum(old, peak)
            sum_ref[kb, :] = sum_ref[kb, :] * jnp.exp2(old - top) + total * jnp.exp2(peak - top)
            top_ref[kb, :] = top

    begin, run = pair_loop(pairs, count, keys_hbm, kbuf, sem, work)
    begin()
    top_ref[...] = jnp.full_like(top_ref, LOW)
    sum_ref[...] = jnp.zeros_like(sum_ref)
    fill_words(tops, lows, words)
    run()
    total = sum_ref[:KB_ALL, :]
    out[...] = jnp.where(total > 0.0, top_ref[:KB_ALL, :] + jnp.log2(total), LOW)


def sums_kernel(pairs, count, keys_hbm, tops, lows, lse, tops_out, lows_out, words, kbuf, acc, sem):
    def work(items, n):
        found = []
        for p, at in items:
            k = kbuf[at].astype(jnp.bfloat16)
            ones = jnp.ones_like(k)
            s = scores_of(words[pairs[p] % NCODE], k, ones)
            post = jnp.exp2(s - lse[pl.ds(pairs[p] // NCODE, 1), :]).astype(jnp.bfloat16)
            wide = jnp.concatenate([k, ones], 1)
            found.append(jnp.dot(post, wide, preferred_element_type=jnp.float32))
        for (p, _), both in zip(items, found):
            acc[jnp.where(p < n, pairs[p] % NCODE, NCODE)] += both

    begin, run = pair_loop(pairs, count, keys_hbm, kbuf, sem, work)
    begin()
    acc[...] = jnp.zeros_like(acc)
    fill_words(tops, lows, words)
    run()
    rows = lax.broadcasted_iota(jnp.int32, (HALF, H), 0)
    lanes = lax.broadcasted_iota(jnp.int32, (HALF, H), 1)
    diag = rows == lanes
    for slot in range(NCODE):
        mass = []
        for half, (ref, to) in enumerate(((tops_out, slot), (lows_out, low_slot(slot)))):
            part = acc[slot, half * HALF : (half + 1) * HALF, :]
            ref[to, :HALF, :] = part[:, :H]
            mass.append(jnp.sum(jnp.where(diag, part[:, H:], 0.0), axis=0, keepdims=True))
        tops_out[slot, HALF:, :] = jnp.concatenate(mass * 4, 0)


SMEM = pl.BlockSpec(memory_space=pltpu.SMEM)
VMEM = pl.BlockSpec(memory_space=pltpu.VMEM)
ANY = pl.BlockSpec(memory_space=pl.ANY)
WORDS = pltpu.VMEM((NCODE, CBLK, 4 * H), jnp.bfloat16)
KBUF = pltpu.VMEM((2 * UNROLL, BLOCK, H), jnp.float32)
KSEM = pltpu.SemaphoreType.DMA((2 * UNROLL,))


def local_logsum(pairs, count, keys, tops, lows):
    return pl.pallas_call(
        logsum_kernel,
        out_shape=jax.ShapeDtypeStruct((KB_ALL, BLOCK), jnp.float32),
        in_specs=[SMEM, SMEM, ANY, VMEM, VMEM],
        out_specs=VMEM,
        scratch_shapes=[
            WORDS,
            KBUF,
            pltpu.VMEM((KB_ALL + 8, BLOCK), jnp.float32),
            pltpu.VMEM((KB_ALL + 8, BLOCK), jnp.float32),
            KSEM,
        ],
        compiler_params=pltpu.CompilerParams(vmem_limit_bytes=40 * 2**20),
        name="local_logsum",
    )(pairs, count, keys, tops, lows)


def local_sums(pairs, count, keys, tops, lows, lse):
    return pl.pallas_call(
        sums_kernel,
        out_shape=(
            jax.ShapeDtypeStruct((NCODE, ROWS, H), jnp.float32),
            jax.ShapeDtypeStruct((NCODE, HALF, H), jnp.float32),
        ),
        in_specs=[SMEM, SMEM, ANY, VMEM, VMEM, VMEM],
        out_specs=(VMEM, VMEM),
        scratch_shapes=[WORDS, KBUF, pltpu.VMEM((NCODE + 1, CBLK, 2 * H), jnp.float32), KSEM],
        compiler_params=pltpu.CompilerParams(vmem_limit_bytes=46 * 2**20),
        name="local_sums",
    )(pairs, count, keys, tops, lows, lse)


def list_pairs(ids, counts, d, x, z):
    kb = lax.broadcasted_iota(jnp.int32, (KB_ALL, LIST_MAX), 0)
    place = lax.broadcasted_iota(jnp.int32, (KB_ALL, LIST_MAX), 1)
    owner = ids // NDP
    take = ((place < counts[:, None]) & (ids % NDP == d)).reshape(-1)
    slot = (owner % NZ - z) % NZ * NX + (owner // NZ - x) % NX
    word = (kb * NCODE + slot).reshape(-1)
    index = jnp.arange(ENTRIES, dtype=jnp.int32)
    ahead = jnp.sum((take[:, None] & (index[:, None] < index[None, :])).astype(jnp.int32), axis=0)
    here = take[:, None] & (ahead[:, None] == index[None, :])
    pairs = jnp.sum(jnp.where(here, word[:, None], 0), axis=0)
    return pairs, jnp.sum(take.astype(jnp.int32)).reshape(1)


def on_device(cached_keys, codebook, block_lists, counts):
    d = lax.axis_index("dp")
    code = lax.axis_index("code")
    x, z = code // NZ, code % NZ
    keys = lax.all_gather(cached_keys.astype(jnp.float32), "dp", axis=0, tiled=True)
    keys = keys.reshape(KB_ALL, BLOCK, H)
    entry = jnp.concatenate([block_lists, counts[:, None], counts[:, None]], 1)
    entries = dp_swap(jnp.broadcast_to(entry[None], (NDP, KB_DEV, 8))).reshape(KB_ALL, 8)
    pairs, count = list_pairs(entries[:, :LIST_MAX], entries[:, LIST_MAX], d, x, z)
    current = lax.dynamic_slice_in_dim(codebook, d * CBLK, CBLK, 0)
    for sweep in range(ITERS):
        tops, lows = gather_words(current)
        part = local_logsum(pairs, count, keys, tops, lows)
        part = dp_swap(part.reshape(NDP, KB_DEV, BLOCK))
        peak = jnp.max(part, axis=0)
        own = peak + jnp.log2(jnp.sum(jnp.exp2(part - peak[None]), axis=0))
        lse = dp_swap(jnp.broadcast_to(own[None], (NDP, KB_DEV, BLOCK))).reshape(KB_ALL, BLOCK)
        tops, lows = local_sums(pairs, count, keys, tops, lows, lse)
        top, low = reduce_sums(tops.reshape(NZ, NX, ROWS, H), lows.reshape(NX, NZ, HALF, H))
        sums = jnp.concatenate([top[:HALF], low], 0)
        mass = jnp.concatenate([top[HALF], top[HALF + 1]], 0)
        current = (sums + current) / (mass[:, None] + 1.0)
    book = dp_swap(jnp.broadcast_to(current[None], (NDP, CBLK, H))).reshape(NDP * CBLK, H)
    return book, (own * LN2).reshape(-1)


def solution(mesh):
    in_specs = (
        P(("dp", "code"), None),
        P("code", None),
        P(("dp", "code"), None),
        P(("dp", "code")),
    )
    out_specs = (P("code", None), P(("dp", "code")))
    return jax.shard_map(
        on_device, mesh=mesh, in_specs=in_specs, out_specs=out_specs, check_vma=False
    )
```

```python
import math

import jax
import jax.numpy as jnp
from jax import lax
from jax.experimental import pallas as pl
from jax.experimental.pallas import tpu as pltpu
from jax.sharding import PartitionSpec as P

CBLK = 256
HALF = CBLK // 2
LIST_MAX = 6
ITERS = 2
BLOCK = 512
H = 128
NX, NZ, NY = 4, 8, 4
NDP = 8
NCODE = NX * NZ
KB_DEV = 8
KB_ALL = NDP * KB_DEV
ENTRIES = KB_ALL * LIST_MAX
ROWS = HALF + 8
SCALE = math.log2(math.e) / math.sqrt(H)
LN2 = math.log(2.0)
LOW = -1e30


def x_step(v, k):
    pairs = [(x * NZ + z, (x + k) % NX * NZ + z) for x in range(NX) for z in range(NZ)]
    return lax.ppermute(v, "code", pairs)


def z_step(v, k):
    pairs = [(x * NZ + z, x * NZ + (z + k) % NZ) for x in range(NX) for z in range(NZ)]
    return lax.ppermute(v, "code", pairs)


def ring_gather(v, n, step):
    h = v.shape[0] // 2
    far = n // 2
    parts = [None] * n
    parts[0] = v
    up, down = v, v
    for s in range(1, far):
        up, down = step(up, 1), step(down, -1)
        parts[n - s], parts[s] = up, down
    a, b = step(up[:h], 1), step(down[h:], -1)
    parts[far] = jnp.concatenate([a, b], 0)
    return parts


def ring_reduce(terms, n, step):
    far = n // 2
    h = terms[0].shape[0] // 2
    a, b = step(terms[far][:h], 1), step(terms[far][h:], -1)
    up = jnp.concatenate([terms[far - 1][:h] + a, terms[far - 1][h:]], 0)
    down = jnp.concatenate([terms[n - far + 1][:h], terms[n - far + 1][h:] + b], 0)
    for s in range(far - 1, 0, -1):
        a, b = step(up, 1), step(down, -1)
        if s > 1:
            up, down = terms[s - 1] + a, terms[n - s + 1] + b
    return terms[0] + a + b


def gather_words(block):
    top, low = block[:HALF], block[HALF:]
    with jax.named_scope("gather_top"):
        mine = jnp.concatenate([top, x_step(top, -1), x_step(top, 2), x_step(top, 1)], 0)
        tops = jnp.concatenate(ring_gather(mine, NZ, z_step), 0)
    with jax.named_scope("gather_low"):
        mine = jnp.concatenate(ring_gather(low, NZ, z_step), 0)
        lows = jnp.concatenate(ring_gather(mine, NX, x_step), 0)
    return tops.reshape(NCODE, HALF, H), lows.reshape(NCODE, HALF, H)


def reduce_sums(tops, lows):
    with jax.named_scope("reduce_top"):
        r = ring_reduce([tops[j].reshape(NX * ROWS, H) for j in range(NZ)], NZ, z_step)
        r = r.reshape(NX, ROWS, H)
        top = r[0] + x_step(r[1], 1) + x_step(r[2], 2) + x_step(r[3], -1)
    with jax.named_scope("reduce_low"):
        r = ring_reduce([lows[i].reshape(NZ * HALF, H) for i in range(NX)], NX, x_step)
        r = r.reshape(NZ, HALF, H)
        low = ring_reduce([r[j] for j in range(NZ)], NZ, z_step)
    return top, low


def dp_swap(v):
    return lax.all_to_all(v, "dp", split_axis=0, concat_axis=0, tiled=True)


UNROLL = 4
PREP = 2


def low_slot(slot):
    return slot % NX * NZ + slot // NX


def fill_words(tops, lows, words, norms):
    @pl.loop(0, NCODE // PREP)
    def _(step):
        for u in range(PREP):
            slot = step * PREP + u
            for half, c in enumerate((tops[slot], lows[low_slot(slot)])):
                rows = pl.ds(half * HALF, HALF)
                s = c * SCALE
                hi = s.astype(jnp.bfloat16)
                words[slot, rows, :H] = hi
                words[slot, rows, H:] = (s - hi.astype(jnp.float32)).astype(jnp.bfloat16)
                norm = jnp.sum(c * c, axis=1, keepdims=True) * (-0.5 * SCALE)
                norms[slot, rows, :] = jnp.broadcast_to(norm, (HALF, H))


def scores_of(words, norms, k):
    twice = jnp.concatenate([k, k], 1)
    s = lax.dot_general(words, twice, (((1,), (1,)), ((), ())), preferred_element_type=jnp.float32)
    return s + jnp.concatenate([norms] * (BLOCK // H), 1)


def pair_loop(pairs, count, keys_hbm, kbuf, sem, work):
    n = count[0]
    steps = (n + (UNROLL - 1)) // UNROLL

    def fetch(step, u):
        at = (step % 2) * UNROLL + u
        kb = pairs[step * UNROLL + u] // NCODE
        return pltpu.make_async_copy(keys_hbm.at[kb], kbuf.at[at], sem.at[at])

    def begin():
        @pl.when(n > 0)
        def _():
            for u in range(UNROLL):
                fetch(0, u).start()

    def run():
        @pl.loop(0, steps)
        def _(step):
            @pl.when(step + 1 < steps)
            def _():
                for u in range(UNROLL):
                    fetch(step + 1, u).start()

            for u in range(UNROLL):
                fetch(step, u).wait()
            work([(step * UNROLL + u, (step % 2) * UNROLL + u) for u in range(UNROLL)], n)

    return begin, run


def logsum_kernel(pairs, count, keys_hbm, tops, lows, out, words, norms, kbuf, top_ref, sum_ref, sem):
    def work(items, n):
        found = []
        for p, at in items:
            k = kbuf[at].astype(jnp.bfloat16)
            slot = pairs[p] % NCODE
            s = scores_of(words[slot], norms[slot], k)
            peak = jnp.max(s, axis=0, keepdims=True)
            found.append((peak, jnp.sum(jnp.exp2(s - peak), axis=0, keepdims=True)))
        for (p, _), (peak, total) in zip(items, found):
            kb = pl.ds(jnp.where(p < n, pairs[p] // NCODE, KB_ALL), 1)
            old = top_ref[kb, :]
            top = jnp.maximum(old, peak)
            sum_ref[kb, :] = sum_ref[kb, :] * jnp.exp2(old - top) + total * jnp.exp2(peak - top)
            top_ref[kb, :] = top

    begin, run = pair_loop(pairs, count, keys_hbm, kbuf, sem, work)
    begin()
    top_ref[...] = jnp.full_like(top_ref, LOW)
    sum_ref[...] = jnp.zeros_like(sum_ref)
    fill_words(tops, lows, words, norms)
    run()
    total = sum_ref[:KB_ALL, :]
    out[...] = jnp.where(total > 0.0, top_ref[:KB_ALL, :] + jnp.log2(total), LOW)


def sums_kernel(pairs, count, keys_hbm, tops, lows, lse, tops_out, lows_out, words, norms, kbuf, acc, sem):
    def work(items, n):
        found = []
        for p, at in items:
            k = kbuf[at].astype(jnp.bfloat16)
            slot = pairs[p] % NCODE
            s = scores_of(words[slot], norms[slot], k)
            post = jnp.exp2(s - lse[pl.ds(pairs[p] // NCODE, 1), :]).astype(jnp.bfloat16)
            wide = jnp.concatenate([k, jnp.ones_like(k)], 1)
            found.append(jnp.dot(post, wide, preferred_element_type=jnp.float32))
        for (p, _), both in zip(items, found):
            acc[jnp.where(p < n, pairs[p] % NCODE, NCODE)] += both

    begin, run = pair_loop(pairs, count, keys_hbm, kbuf, sem, work)
    begin()
    acc[...] = jnp.zeros_like(acc)
    fill_words(tops, lows, words, norms)
    run()
    rows = lax.broadcasted_iota(jnp.int32, (HALF, H), 0)
    lanes = lax.broadcasted_iota(jnp.int32, (HALF, H), 1)
    diag = rows == lanes
    for slot in range(NCODE):
        mass = []
        for half, (ref, to) in enumerate(((tops_out, slot), (lows_out, low_slot(slot)))):
            part = acc[slot, half * HALF : (half + 1) * HALF, :]
            ref[to, :HALF, :] = part[:, :H]
            mass.append(jnp.sum(jnp.where(diag, part[:, H:], 0.0), axis=0, keepdims=True))
        tops_out[slot, HALF:, :] = jnp.concatenate(mass * 4, 0)


SMEM = pl.BlockSpec(memory_space=pltpu.SMEM)
VMEM = pl.BlockSpec(memory_space=pltpu.VMEM)
ANY = pl.BlockSpec(memory_space=pl.ANY)
WORDS = pltpu.VMEM((NCODE, CBLK, 2 * H), jnp.bfloat16)
NORMS = pltpu.VMEM((NCODE, CBLK, H), jnp.float32)
KBUF = pltpu.VMEM((2 * UNROLL, BLOCK, H), jnp.float32)
KSEM = pltpu.SemaphoreType.DMA((2 * UNROLL,))


def local_logsum(pairs, count, keys, tops, lows):
    return pl.pallas_call(
        logsum_kernel,
        out_shape=jax.ShapeDtypeStruct((KB_ALL, BLOCK), jnp.float32),
        in_specs=[SMEM, SMEM, ANY, VMEM, VMEM],
        out_specs=VMEM,
        scratch_shapes=[
            WORDS,
            NORMS,
            KBUF,
            pltpu.VMEM((KB_ALL + 8, BLOCK), jnp.float32),
            pltpu.VMEM((KB_ALL + 8, BLOCK), jnp.float32),
            KSEM,
        ],
        compiler_params=pltpu.CompilerParams(vmem_limit_bytes=40 * 2**20),
        name="local_logsum",
    )(pairs, count, keys, tops, lows)


def local_sums(pairs, count, keys, tops, lows, lse):
    return pl.pallas_call(
        sums_kernel,
        out_shape=(
            jax.ShapeDtypeStruct((NCODE, ROWS, H), jnp.float32),
            jax.ShapeDtypeStruct((NCODE, HALF, H), jnp.float32),
        ),
        in_specs=[SMEM, SMEM, ANY, VMEM, VMEM, VMEM],
        out_specs=(VMEM, VMEM),
        scratch_shapes=[WORDS, NORMS, KBUF, pltpu.VMEM((NCODE + 1, CBLK, 2 * H), jnp.float32), KSEM],
        compiler_params=pltpu.CompilerParams(vmem_limit_bytes=46 * 2**20),
        name="local_sums",
    )(pairs, count, keys, tops, lows, lse)


def list_pairs(ids, counts, d, x, z):
    kb = lax.broadcasted_iota(jnp.int32, (KB_ALL, LIST_MAX), 0)
    place = lax.broadcasted_iota(jnp.int32, (KB_ALL, LIST_MAX), 1)
    owner = ids // NDP
    take = ((place < counts[:, None]) & (ids % NDP == d)).reshape(-1)
    slot = (owner % NZ - z) % NZ * NX + (owner // NZ - x) % NX
    word = (kb * NCODE + slot).reshape(-1)
    index = jnp.arange(ENTRIES, dtype=jnp.int32)
    ahead = jnp.sum((take[:, None] & (index[:, None] < index[None, :])).astype(jnp.int32), axis=0)
    here = take[:, None] & (ahead[:, None] == index[None, :])
    pairs = jnp.sum(jnp.where(here, word[:, None], 0), axis=0)
    return pairs, jnp.sum(take.astype(jnp.int32)).reshape(1)


def on_device(cached_keys, codebook, block_lists, counts):
    d = lax.axis_index("dp")
    code = lax.axis_index("code")
    x, z = code // NZ, code % NZ
    keys = lax.all_gather(cached_keys.astype(jnp.float32), "dp", axis=0, tiled=True)
    keys = keys.reshape(KB_ALL, BLOCK, H)
    entry = jnp.concatenate([block_lists, counts[:, None], counts[:, None]], 1)
    entries = dp_swap(jnp.broadcast_to(entry[None], (NDP, KB_DEV, 8))).reshape(KB_ALL, 8)
    pairs, count = list_pairs(entries[:, :LIST_MAX], entries[:, LIST_MAX], d, x, z)
    current = lax.dynamic_slice_in_dim(codebook, d * CBLK, CBLK, 0)
    for sweep in range(ITERS):
        tops, lows = gather_words(current)
        part = local_logsum(pairs, count, keys, tops, lows)
        part = dp_swap(part.reshape(NDP, KB_DEV, BLOCK))
        peak = jnp.max(part, axis=0)
        own = peak + jnp.log2(jnp.sum(jnp.exp2(part - peak[None]), axis=0))
        lse = dp_swap(jnp.broadcast_to(own[None], (NDP, KB_DEV, BLOCK))).reshape(KB_ALL, BLOCK)
        tops, lows = local_sums(pairs, count, keys, tops, lows, lse)
        top, low = reduce_sums(tops.reshape(NZ, NX, ROWS, H), lows.reshape(NX, NZ, HALF, H))
        sums = jnp.concatenate([top[:HALF], low], 0)
        mass = jnp.concatenate([top[HALF], top[HALF + 1]], 0)
        current = (sums + current) / (mass[:, None] + 1.0)
    book = dp_swap(jnp.broadcast_to(current[None], (NDP, CBLK, H))).reshape(NDP * CBLK, H)
    return book, (own * LN2).reshape(-1)


def solution(mesh):
    in_specs = (
        P(("dp", "code"), None),
        P("code", None),
        P(("dp", "code"), None),
        P(("dp", "code")),
    )
    out_specs = (P("code", None), P(("dp", "code")))
    return jax.shard_map(
        on_device, mesh=mesh, in_specs=in_specs, out_specs=out_specs, check_vma=False
    )
```

```python
import math

import jax
import jax.numpy as jnp
from jax import lax
from jax.experimental import pallas as pl
from jax.experimental.pallas import tpu as pltpu
from jax.sharding import PartitionSpec as P

CBLK = 256
HALF = CBLK // 2
LIST_MAX = 6
ITERS = 2
BLOCK = 512
H = 128
NX, NZ, NY = 4, 8, 4
NDP = 8
NCODE = NX * NZ
KB_DEV = 8
KB_ALL = NDP * KB_DEV
ENTRIES = KB_ALL * LIST_MAX
ROWS = HALF + 8
SCALE = math.log2(math.e) / math.sqrt(H)
LN2 = math.log(2.0)
LOW = -1e30


def x_step(v, k):
    pairs = [(x * NZ + z, (x + k) % NX * NZ + z) for x in range(NX) for z in range(NZ)]
    return lax.ppermute(v, "code", pairs)


def z_step(v, k):
    pairs = [(x * NZ + z, x * NZ + (z + k) % NZ) for x in range(NX) for z in range(NZ)]
    return lax.ppermute(v, "code", pairs)


def ring_gather(v, n, step):
    h = v.shape[0] // 2
    far = n // 2
    parts = [None] * n
    parts[0] = v
    up, down = v, v
    for s in range(1, far):
        up, down = step(up, 1), step(down, -1)
        parts[n - s], parts[s] = up, down
    a, b = step(up[:h], 1), step(down[h:], -1)
    parts[far] = jnp.concatenate([a, b], 0)
    return parts


def ring_reduce(terms, n, step):
    far = n // 2
    h = terms[0].shape[0] // 2
    a, b = step(terms[far][:h], 1), step(terms[far][h:], -1)
    up = jnp.concatenate([terms[far - 1][:h] + a, terms[far - 1][h:]], 0)
    down = jnp.concatenate([terms[n - far + 1][:h], terms[n - far + 1][h:] + b], 0)
    for s in range(far - 1, 0, -1):
        a, b = step(up, 1), step(down, -1)
        if s > 1:
            up, down = terms[s - 1] + a, terms[n - s + 1] + b
    return terms[0] + a + b


def gather_words(block):
    top, low = block[:HALF], block[HALF:]
    with jax.named_scope("gather_top"):
        mine = jnp.concatenate([top, x_step(top, -1), x_step(top, 2), x_step(top, 1)], 0)
        tops = jnp.concatenate(ring_gather(mine, NZ, z_step), 0)
    with jax.named_scope("gather_low"):
        mine = jnp.concatenate(ring_gather(low, NZ, z_step), 0)
        lows = jnp.concatenate(ring_gather(mine, NX, x_step), 0)
    return tops.reshape(NCODE, HALF, H), lows.reshape(NCODE, HALF, H)


def reduce_sums(tops, lows):
    with jax.named_scope("reduce_top"):
        r = ring_reduce([tops[j].reshape(NX * ROWS, H) for j in range(NZ)], NZ, z_step)
        r = r.reshape(NX, ROWS, H)
        top = r[0] + x_step(r[1], 1) + x_step(r[2], 2) + x_step(r[3], -1)
    with jax.named_scope("reduce_low"):
        r = ring_reduce([lows[i].reshape(NZ * HALF, H) for i in range(NX)], NX, x_step)
        r = r.reshape(NZ, HALF, H)
        low = ring_reduce([r[j] for j in range(NZ)], NZ, z_step)
    return top, low


def dp_swap(v):
    return lax.all_to_all(v, "dp", split_axis=0, concat_axis=0, tiled=True)


UNROLL = 6
PREP = 2


def low_slot(slot):
    return slot % NX * NZ + slot // NX


def fill_words(tops, lows, words, norms):
    @pl.loop(0, NCODE // PREP)
    def _(step):
        for u in range(PREP):
            slot = step * PREP + u
            for half, c in enumerate((tops[slot], lows[low_slot(slot)])):
                rows = pl.ds(half * HALF, HALF)
                s = c * SCALE
                hi = s.astype(jnp.bfloat16)
                words[slot, rows, :H] = hi
                words[slot, rows, H:] = (s - hi.astype(jnp.float32)).astype(jnp.bfloat16)
                norm = jnp.sum(c * c, axis=1, keepdims=True) * (-0.5 * SCALE)
                norms[slot, rows, :] = jnp.broadcast_to(norm, (HALF, H))


def scores_of(words, norms, k):
    twice = jnp.concatenate([k, k], 1)
    s = lax.dot_general(words, twice, (((1,), (1,)), ((), ())), preferred_element_type=jnp.float32)
    return s + jnp.concatenate([norms] * (BLOCK // H), 1)


def pair_loop(pairs, count, keys_hbm, kbuf, sem, work):
    n = count[0]
    steps = (n + (UNROLL - 1)) // UNROLL

    def fetch(step, u):
        at = (step % 2) * UNROLL + u
        kb = pairs[step * UNROLL + u] // NCODE
        return pltpu.make_async_copy(keys_hbm.at[kb], kbuf.at[at], sem.at[at])

    def begin():
        @pl.when(n > 0)
        def _():
            for u in range(UNROLL):
                fetch(0, u).start()

    def run():
        @pl.loop(0, steps)
        def _(step):
            @pl.when(step + 1 < steps)
            def _():
                for u in range(UNROLL):
                    fetch(step + 1, u).start()

            for u in range(UNROLL):
                fetch(step, u).wait()
            work([(step * UNROLL + u, (step % 2) * UNROLL + u) for u in range(UNROLL)], n)

    return begin, run


def logsum_kernel(pairs, count, keys_hbm, tops, lows, out, words, norms, kbuf, top_ref, sum_ref, sem):
    def work(items, n):
        found = []
        for p, at in items:
            k = kbuf[at].astype(jnp.bfloat16)
            slot = pairs[p] % NCODE
            s = scores_of(words[slot], norms[slot], k)
            peak = jnp.max(s, axis=0, keepdims=True)
            found.append((peak, jnp.sum(jnp.exp2(s - peak), axis=0, keepdims=True)))
        for (p, _), (peak, total) in zip(items, found):
            kb = pl.ds(jnp.where(p < n, pairs[p] // NCODE, KB_ALL), 1)
            old = top_ref[kb, :]
            top = jnp.maximum(old, peak)
            sum_ref[kb, :] = sum_ref[kb, :] * jnp.exp2(old - top) + total * jnp.exp2(peak - top)
            top_ref[kb, :] = top

    begin, run = pair_loop(pairs, count, keys_hbm, kbuf, sem, work)
    begin()
    top_ref[...] = jnp.full_like(top_ref, LOW)
    sum_ref[...] = jnp.zeros_like(sum_ref)
    fill_words(tops, lows, words, norms)
    run()
    total = sum_ref[:KB_ALL, :]
    out[...] = jnp.where(total > 0.0, top_ref[:KB_ALL, :] + jnp.log2(total), LOW)


def sums_kernel(pairs, count, keys_hbm, tops, lows, lse, tops_out, lows_out, words, norms, kbuf, acc, sem):
    def work(items, n):
        found = []
        for p, at in items:
            k = kbuf[at].astype(jnp.bfloat16)
            slot = pairs[p] % NCODE
            s = scores_of(words[slot], norms[slot], k)
            post = jnp.exp2(s - lse[pl.ds(pairs[p] // NCODE, 1), :]).astype(jnp.bfloat16)
            wide = jnp.concatenate([k, jnp.ones_like(k)], 1)
            found.append(jnp.dot(post, wide, preferred_element_type=jnp.float32))
        for (p, _), both in zip(items, found):
            acc[jnp.where(p < n, pairs[p] % NCODE, NCODE)] += both

    begin, run = pair_loop(pairs, count, keys_hbm, kbuf, sem, work)
    begin()
    acc[...] = jnp.zeros_like(acc)
    fill_words(tops, lows, words, norms)
    run()
    rows = lax.broadcasted_iota(jnp.int32, (HALF, H), 0)
    lanes = lax.broadcasted_iota(jnp.int32, (HALF, H), 1)
    diag = rows == lanes
    for slot in range(NCODE):
        mass = []
        for half, (ref, to) in enumerate(((tops_out, slot), (lows_out, low_slot(slot)))):
            part = acc[slot, half * HALF : (half + 1) * HALF, :]
            ref[to, :HALF, :] = part[:, :H]
            mass.append(jnp.sum(jnp.where(diag, part[:, H:], 0.0), axis=0, keepdims=True))
        tops_out[slot, HALF:, :] = jnp.concatenate(mass * 4, 0)


SMEM = pl.BlockSpec(memory_space=pltpu.SMEM)
VMEM = pl.BlockSpec(memory_space=pltpu.VMEM)
ANY = pl.BlockSpec(memory_space=pl.ANY)
WORDS = pltpu.VMEM((NCODE, CBLK, 2 * H), jnp.bfloat16)
NORMS = pltpu.VMEM((NCODE, CBLK, H), jnp.float32)
KBUF = pltpu.VMEM((2 * UNROLL, BLOCK, H), jnp.float32)
KSEM = pltpu.SemaphoreType.DMA((2 * UNROLL,))


def local_logsum(pairs, count, keys, tops, lows):
    return pl.pallas_call(
        logsum_kernel,
        out_shape=jax.ShapeDtypeStruct((KB_ALL, BLOCK), jnp.float32),
        in_specs=[SMEM, SMEM, ANY, VMEM, VMEM],
        out_specs=VMEM,
        scratch_shapes=[
            WORDS,
            NORMS,
            KBUF,
            pltpu.VMEM((KB_ALL + 8, BLOCK), jnp.float32),
            pltpu.VMEM((KB_ALL + 8, BLOCK), jnp.float32),
            KSEM,
        ],
        compiler_params=pltpu.CompilerParams(vmem_limit_bytes=40 * 2**20),
        name="local_logsum",
    )(pairs, count, keys, tops, lows)


def local_sums(pairs, count, keys, tops, lows, lse):
    return pl.pallas_call(
        sums_kernel,
        out_shape=(
            jax.ShapeDtypeStruct((NCODE, ROWS, H), jnp.float32),
            jax.ShapeDtypeStruct((NCODE, HALF, H), jnp.float32),
        ),
        in_specs=[SMEM, SMEM, ANY, VMEM, VMEM, VMEM],
        out_specs=(VMEM, VMEM),
        scratch_shapes=[WORDS, NORMS, KBUF, pltpu.VMEM((NCODE + 1, CBLK, 2 * H), jnp.float32), KSEM],
        compiler_params=pltpu.CompilerParams(vmem_limit_bytes=46 * 2**20),
        name="local_sums",
    )(pairs, count, keys, tops, lows, lse)


def list_pairs(ids, counts, d, x, z):
    kb = lax.broadcasted_iota(jnp.int32, (KB_ALL, LIST_MAX), 0)
    place = lax.broadcasted_iota(jnp.int32, (KB_ALL, LIST_MAX), 1)
    owner = ids // NDP
    take = ((place < counts[:, None]) & (ids % NDP == d)).reshape(-1)
    slot = (owner % NZ - z) % NZ * NX + (owner // NZ - x) % NX
    word = (kb * NCODE + slot).reshape(-1)
    index = jnp.arange(ENTRIES, dtype=jnp.int32)
    ahead = jnp.sum((take[:, None] & (index[:, None] < index[None, :])).astype(jnp.int32), axis=0)
    here = take[:, None] & (ahead[:, None] == index[None, :])
    pairs = jnp.sum(jnp.where(here, word[:, None], 0), axis=0)
    return pairs, jnp.sum(take.astype(jnp.int32)).reshape(1)


def on_device(cached_keys, codebook, block_lists, counts):
    d = lax.axis_index("dp")
    code = lax.axis_index("code")
    x, z = code // NZ, code % NZ
    keys = lax.all_gather(cached_keys.astype(jnp.float32), "dp", axis=0, tiled=True)
    keys = keys.reshape(KB_ALL, BLOCK, H)
    entry = jnp.concatenate([block_lists, counts[:, None], counts[:, None]], 1)
    entries = dp_swap(jnp.broadcast_to(entry[None], (NDP, KB_DEV, 8))).reshape(KB_ALL, 8)
    pairs, count = list_pairs(entries[:, :LIST_MAX], entries[:, LIST_MAX], d, x, z)
    current = lax.dynamic_slice_in_dim(codebook, d * CBLK, CBLK, 0)
    for sweep in range(ITERS):
        tops, lows = gather_words(current)
        part = local_logsum(pairs, count, keys, tops, lows)
        part = dp_swap(part.reshape(NDP, KB_DEV, BLOCK))
        peak = jnp.max(part, axis=0)
        own = peak + jnp.log2(jnp.sum(jnp.exp2(part - peak[None]), axis=0))
        lse = dp_swap(jnp.broadcast_to(own[None], (NDP, KB_DEV, BLOCK))).reshape(KB_ALL, BLOCK)
        tops, lows = local_sums(pairs, count, keys, tops, lows, lse)
        top, low = reduce_sums(tops.reshape(NZ, NX, ROWS, H), lows.reshape(NX, NZ, HALF, H))
        sums = jnp.concatenate([top[:HALF], low], 0)
        mass = jnp.concatenate([top[HALF], top[HALF + 1]], 0)
        current = (sums + current) / (mass[:, None] + 1.0)
    book = dp_swap(jnp.broadcast_to(current[None], (NDP, CBLK, H))).reshape(NDP * CBLK, H)
    return book, (own * LN2).reshape(-1)


def solution(mesh):
    in_specs = (
        P(("dp", "code"), None),
        P("code", None),
        P(("dp", "code"), None),
        P(("dp", "code")),
    )
    out_specs = (P("code", None), P(("dp", "code")))
    return jax.shard_map(
        on_device, mesh=mesh, in_specs=in_specs, out_specs=out_specs, check_vma=False
    )
```
